32 devices in a mesh: row: 4 (over z), col: 8 (over y, x, core).
Axes of the slice: x: 2, y: 2, z: 4, core: 2. Of those that a mesh axis runs over, the one named last changes fastest.
Arguments:
- page_tokens: bfloat16 [512, 7168], P('row', 'col'), may hold values from -6 to 6
- weight_in: bfloat16 [7168, 28672], P('col', 'row'), may hold values from -0.0625 to 0.0625
- weight_out: bfloat16 [28672, 7168], P('row', 'col'), may hold values from -0.03125 to 0.03125
- upstream: bfloat16 [512, 7168], P('row', 'col'), may hold values from -3 to 3
Outputs:
- block_out: bfloat16 [512, 7168], P('row', 'col')
- grad_tokens: bfloat16 [512, 7168], P('row', 'col')
- grad_weight_in: bfloat16 [7168, 28672], P('col', 'row')
- grad_weight_out: bfloat16 [28672, 7168], P('row', 'col')
The draws below stay inside these ranges and needn't reach their ends.
All inputs are finite; a program needn't handle non-finite values.
Results may differ from the reference program's by a relative error of at most 0.028.
Values may be sent and summed in bfloat16 or wider, within the bound.
A program may use at most 128 MiB of HBM per device.

```python
import jax
import jax.numpy as jnp
from jax import lax

D = 7168
FF = 28672
TOKENS = 512
N_ROW = 4
N_COL = 8


def block_levels(stream_key, dims, shards, smallest, top_value):
    factor_of = 1.0
    for axis_at, shards_of in shards:
        steps = jax.random.uniform(jax.random.fold_in(jax.random.fold_in(stream_key, 6), axis_at), (shards_of,), jnp.float32, smallest / len(shards), top_value / len(shards))
        factor_of = factor_of * jnp.repeat(jnp.exp(steps), dims[axis_at] // shards_of).reshape((-1,) + (1,) * (len(dims) - 1 - axis_at))
    return factor_of


def gaussian(own_key, dims, deviation, most, split=(), dtype=jnp.bfloat16):
    loudness = block_levels(own_key, dims, split, -0.22, 0.18) if split else 1.0
    values = jax.random.normal(own_key, dims, jnp.float32) * deviation * loudness
    return jnp.minimum(jnp.maximum(values, -most), most).astype(dtype)


def setup_inputs(seed: int = 0) -> dict:
    arg_keys = jax.random.split(jax.random.key(seed), 5)
    return {
        "page_tokens": gaussian(arg_keys[0], (TOKENS, D), 1.0, 6.0, ((0, 4), (1, 8))),
        "weight_in": gaussian(arg_keys[1], (D, FF), D ** -0.5, 0.0625, ((0, 8), (1, 4))),
        "weight_out": gaussian(arg_keys[2], (FF, D), FF ** -0.5, 0.03125, ((0, 4), (1, 8))),
        "upstream": gaussian(arg_keys[3], (TOKENS, D), 0.5, 3.0, ((0, 4), (1, 8))),
    }


def activate(values):
    return 0.5 * values * (1.0 + jnp.tanh(0.7978845608 * (values + 0.044715 * values * values * values)))

def partial_sums(left, right, parts):
    stride = left.shape[1] // parts
    total = jnp.zeros((left.shape[0], right.shape[1]), jnp.float32)
    for index in range(parts):
        piece = jnp.dot(left[:, index * stride:(index + 1) * stride], right[index * stride:(index + 1) * stride, :], preferred_element_type=jnp.float32)
        piece = lax.optimization_barrier(piece.astype(jnp.bfloat16))
        total = total + piece.astype(jnp.float32)
    return total

def reference(page_tokens, weight_in, weight_out, upstream):
    hidden_pre = partial_sums(page_tokens, weight_in, N_COL)
    active = activate(hidden_pre).astype(jnp.bfloat16)
    block_out = partial_sums(active, weight_out, N_ROW).astype(jnp.bfloat16)
    grad_active = partial_sums(upstream, weight_out.T, N_COL)
    grad_hidden = jax.vjp(activate, hidden_pre)[1](grad_active)[0].astype(jnp.bfloat16)
    grad_tokens = partial_sums(grad_hidden, weight_in.T, N_ROW).astype(jnp.bfloat16)
    grad_weight_in = jnp.dot(page_tokens.T, grad_hidden, preferred_element_type=jnp.float32).astype(jnp.bfloat16)
    grad_weight_out = jnp.dot(active.T, upstream, preferred_element_type=jnp.float32).astype(jnp.bfloat16)
    return (block_out, grad_tokens, grad_weight_in, grad_weight_out)
```

```python
import functools

import jax
import jax.numpy as jnp
from jax import lax
from jax.experimental import pallas as pl
from jax.experimental.pallas import tpu as pltpu
from jax.sharding import PartitionSpec as P

MESH = pl.DeviceIdType.MESH
RING = 8
BF = jnp.bfloat16
F32 = jnp.float32


def activate(values):
    return (
        0.5
        * values
        * (1.0 + jnp.tanh(0.7978845608 * (values + 0.044715 * values * values * values)))
    )


def slope(values):
    square = values * values
    bend = jnp.tanh(0.7978845608 * (values + 0.044715 * square * values))
    return 0.5 * (1.0 + bend) + 0.5 * values * (1.0 - bend * bend) * (
        0.7978845608 * (1.0 + 0.134145 * square)
    )


def contract_last(left, right):
    return lax.dot_general(left, right, (((1,), (1,)), ((), ())), preferred_element_type=F32)


def contract_first(left, right):
    return lax.dot_general(left, right, (((0,), (0,)), ((), ())), preferred_element_type=F32)


def kernel(
    n_row,
    n_col,
    tokens_ref,
    upstream_ref,
    weight_in,
    weight_out,
    block_part,
    token_part,
    active_out,
    hidden_out,
    features_out,
    upstream_out,
    *scratch,
):
    levels = n_col.bit_length() - 1
    piles = scratch[: levels]
    landed = scratch[levels : 2 * levels]
    (
        gathered,
        held_in,
        held_out,
        features,
        upstream,
        pre,
        total,
        stage_send,
        stage_recv,
        spread_send,
        spread_recv,
        row_send,
        row_recv,
        weight_sem,
        out_sem,
        side_sem,
    ) = scratch[2 * levels :]
    chunks, depth, width = held_in.shape
    tall = features.shape[0]
    rows = tokens_ref.shape[0]
    steps = 2 * chunks
    here = lax.axis_index("row")
    me = lax.axis_index("col")

    bits = [(me // 2**j) % 2 for j in range(levels)]
    strides = [2**j for j in range(levels)]
    if levels == 3:
        core, bx, by = bits
        bits = [core, bx * (1 - core) + by * core, by * (1 - core) + bx * core]
        strides = [1, 2 + 2 * core, 4 - 2 * core]
    mates = [me + s * (1 - 2 * b) for s, b in zip(strides, bits)]
    sizes = [tall >> (j + 1) for j in range(levels)]
    starts = [0]
    for j in range(levels):
        starts.append(starts[-1] + bits[j] * sizes[j])

    barrier = pltpu.get_barrier_semaphore()
    for mate in mates:
        pl.semaphore_signal(barrier, inc=1, device_id=(here, mate), device_id_type=MESH)

    @pl.when(here > 0)
    def _():
        pl.semaphore_signal(barrier, inc=1, device_id=(here - 1, me), device_id_type=MESH)

    @pl.when(here < n_row - 1)
    def _():
        pl.semaphore_signal(barrier, inc=1, device_id=(here + 1, me), device_id_type=MESH)

    def load_in(k):
        return pltpu.make_async_copy(
            weight_in.at[:, pl.ds(pl.multiple_of(k * width, width), width)],
            held_in.at[k],
            weight_sem.at[0, k],
        )

    def load_out(k):
        return pltpu.make_async_copy(
            weight_out.at[pl.ds(pl.multiple_of(k * width, width), width), :],
            held_out.at[k],
            weight_sem.at[1, k],
        )

    @pl.loop(0, chunks)
    def _(k):
        load_in(k).start()

    sources = (tokens_ref, upstream_ref)
    whole = (features, upstream)

    def block_of(kind, origin):
        return whole[kind].at[pl.ds(pl.multiple_of(origin * rows, rows), rows), :]

    def hop(kind, way, dist):
        origin = here - dist if way == 0 else here + dist
        goal = here + 1 if way == 0 else here - 1
        source = sources[kind] if dist == 0 else block_of(kind, origin)
        return pltpu.make_async_remote_copy(
            src_ref=source,
            dst_ref=block_of(kind, origin),
            send_sem=row_send.at[kind, way, dist],
            recv_sem=row_recv.at[kind, way, dist],
            device_id=(goal, me),
            device_id_type=MESH,
        )

    def sends(way, dist):
        if way == 0:
            return (here >= dist) & (here < n_row - 1)
        return (here < n_row - dist) & (here > 0)

    def takes(way, dist):
        return here >= dist + 1 if way == 0 else here < n_row - dist - 1

    def arrive(kind, dist):
        for way in (0, 1):

            @pl.when(takes(way, dist))
            def _(way=way):
                origin = here - dist - 1 if way == 0 else here + dist + 1
                pltpu.make_async_remote_copy(
                    src_ref=block_of(kind, origin),
                    dst_ref=block_of(kind, origin),
                    send_sem=row_send.at[kind, way, dist],
                    recv_sem=row_recv.at[kind, way, dist],
                    device_id=(here - 1 if way == 0 else here + 1, me),
                    device_id_type=MESH,
                ).wait_recv()

            if dist + 1 < n_row - 1:

                @pl.when(sends(way, dist + 1))
                def _(way=way):
                    hop(kind, way, dist + 1).start()

    neighbours = jnp.where(here > 0, 1, 0) + jnp.where(here < n_row - 1, 1, 0)
    pl.semaphore_wait(barrier, levels + neighbours)

    for kind in (0, 1):
        for way in (0, 1):

            @pl.when(sends(way, 0))
            def _(kind=kind, way=way):
                hop(kind, way, 0).start()

    @pl.loop(0, chunks)
    def _(k):
        load_out(k).start()

    own = pl.ds(pl.multiple_of(here * rows, rows), rows)
    features[own, :] = tokens_ref[...]
    upstream[own, :] = upstream_ref[...]
    for dist in range(n_row - 1):
        arrive(0, dist)
    pltpu.make_async_copy(features, features_out, side_sem.at[0]).start()

    def stage(j, t):
        other = pl.multiple_of((1 - bits[j]) * sizes[j], sizes[j])
        return pltpu.make_async_remote_copy(
            src_ref=piles[j].at[lax.rem(t, 2), pl.ds(other, sizes[j]), :],
            dst_ref=landed[j].at[lax.rem(t, RING)],
            send_sem=stage_send.at[j, lax.rem(t, 2)],
            recv_sem=stage_recv.at[j, lax.rem(t, RING)],
            device_id=(here, mates[j]),
            device_id_type=MESH,
        )

    def spread(j, t, mine=True):
        at = starts[j + 1] if mine else starts[j] + (1 - bits[j]) * sizes[j]
        view = gathered.at[lax.rem(t, RING), pl.ds(pl.multiple_of(at, sizes[j]), sizes[j]), :]
        return pltpu.make_async_remote_copy(
            src_ref=view,
            dst_ref=view,
            send_sem=spread_send.at[j, lax.rem(t, 2)],
            recv_sem=spread_recv.at[j, lax.rem(t, RING)],
            device_id=(here, mates[j]),
            device_id_type=MESH,
        )

    def columns(k):
        return pl.ds(pl.multiple_of(k * width, width), width)

    def put_active(t):
        return pltpu.make_async_copy(
            gathered.at[lax.rem(t, RING)], active_out.at[:, columns(t)], out_sem.at[lax.rem(t, 2)]
        )

    def put_hidden(t):
        return pltpu.make_async_copy(
            gathered.at[lax.rem(t, RING)],
            hidden_out.at[:, columns(t - chunks)],
            out_sem.at[lax.rem(t, 2)],
        )

    tile = min(256, tall)

    def during(t, act):
        pl.when((t >= 0) & (t < steps))(act)

    def produce(t):
        slot = lax.rem(t, 2)

        @pl.when(t < chunks)
        def _():
            load_in(t).wait()

            @pl.loop(0, tall // tile)
            def _(r):
                at = pl.ds(pl.multiple_of(r * tile, tile), tile)
                piles[0][slot, at, :] = jnp.dot(
                    features[at, :], held_in[t], preferred_element_type=F32
                ).astype(BF)

        @pl.when(t >= chunks)
        def _():
            @pl.loop(0, tall // tile)
            def _(r):
                at = pl.ds(pl.multiple_of(r * tile, tile), tile)
                piles[0][slot, at, :] = contract_last(
                    upstream[at, :], held_out[t - chunks]
                ).astype(BF)

        stage(0, t).start()

    def fold(j, t):
        copy = stage(j, t)
        copy.wait_send()
        copy.wait_recv()
        slot, ring = lax.rem(t, 2), lax.rem(t, RING)
        part = min(32, sizes[j])
        keep = bits[j] * sizes[j]

        if j < levels - 1:
            def combine(r):
                at = pl.ds(pl.multiple_of(r * part, part), part)
                held = pl.ds(pl.multiple_of(keep + r * part, part), part)
                piles[j + 1][slot, at, :] = (
                    piles[j][slot, held, :].astype(F32) + landed[j][ring, at, :].astype(F32)
                ).astype(BF)

            count = sizes[j + 1] // part
            other = (1 - bits[j + 1]) * count

            @pl.loop(0, count)
            def _(r):
                combine(other + r)

            stage(j + 1, t).start()
            mine = bits[j + 1] * count

            @pl.loop(0, count)
            def _(r):
                combine(mine + r)
        else:
            k = lax.rem(t, chunks)

            @pl.loop(0, sizes[j] // part)
            def _(r):
                at = pl.ds(pl.multiple_of(r * part, part), part)
                held = pl.ds(pl.multiple_of(keep + r * part, part), part)
                target = pl.ds(pl.multiple_of(starts[levels] + r * part, part), part)
                value = piles[j][slot, held, :].astype(F32) + landed[j][ring, at, :].astype(F32)

                @pl.when(t < chunks)
                def _():
                    pre[k, at, :] = value
                    gathered[ring, target, :] = activate(value).astype(BF)

                @pl.when(t >= chunks)
                def _():
                    gathered[ring, target, :] = (value * slope(pre[k, at, :])).astype(BF)

            spread(j, t).start()

    def gather(j, t):
        spread(j, t).wait_send()
        spread(j, t, mine=False).wait_recv()
        spread(j - 1, t).start()

    def consume(t):
        spread(0, t).wait_send()
        spread(0, t, mine=False).wait_recv()
        ring = lax.rem(t, RING)
        k = lax.rem(t, chunks)

        @pl.when(k == 0)
        def _():
            total[...] = jnp.zeros_like(total)

        @pl.when(t < chunks)
        def _():
            put_active(t).start()
            load_out(t).wait()

            @pl.loop(0, tall // tile)
            def _(r):
                at = pl.ds(pl.multiple_of(r * tile, tile), tile)
                total[at, :] += jnp.dot(
                    gathered[ring, at, :], held_out[t], preferred_element_type=F32
                )

        @pl.when(t >= chunks)
        def _():
            put_hidden(t).start()

            @pl.loop(0, tall // tile)
            def _(r):
                at = pl.ds(pl.multiple_of(r * tile, tile), tile)
                total[at, :] += contract_last(gathered[ring, at, :], held_in[t - chunks])

        @pl.when(t == chunks - 1)
        def _():
            block_part[...] = total[...].astype(BF)

        @pl.when(t == steps - 1)
        def _():
            token_part[...] = total[...].astype(BF)

    def written(t):
        @pl.when(t < chunks)
        def _():
            put_active(t).wait()

        @pl.when(t >= chunks)
        def _():
            put_hidden(t).wait()

    lag = 2 * levels

    @pl.loop(0, steps + lag + 1)
    def _(i):
        during(i - lag - 1, lambda: written(i - lag - 1))
        during(i - lag, lambda: consume(i - lag))
        for j in range(1, levels):
            t = i - lag + j
            during(t, functools.partial(gather, j, t))
        for j in range(levels - 1, -1, -1):
            t = i - j - 1
            during(t, functools.partial(fold, j, t))
        during(i, lambda: produce(i))
        for dist in range(n_row - 1):

            @pl.when(i == dist)
            def _(dist=dist):
                arrive(1, dist)

    side = pltpu.make_async_copy(upstream, upstream_out, side_sem.at[1])
    side.start()
    side.wait()
    pltpu.make_async_copy(features, features_out, side_sem.at[0]).wait()
    for kind in (0, 1):
        for dist in range(n_row - 1):
            for way in (0, 1):

                @pl.when(sends(way, dist))
                def _(kind=kind, way=way, dist=dist):
                    hop(kind, way, dist).wait_send()


def encode(n_row, n_col, page_tokens, upstream, weight_in, weight_out):
    rows, depth = page_tokens.shape
    hidden = weight_in.shape[1]
    tall = rows * n_row
    levels = n_col.bit_length() - 1
    chunks = 14
    width = hidden // chunks
    vmem = pl.BlockSpec(memory_space=pltpu.VMEM)
    anywhere = pl.BlockSpec(memory_space=pl.ANY)
    dma = pltpu.SemaphoreType.DMA
    shape = jax.ShapeDtypeStruct
    flops = 8 * tall * depth * hidden
    return pl.pallas_call(
        functools.partial(kernel, n_row, n_col),
        out_shape=[
            shape((tall, depth), BF),
            shape((tall, depth), BF),
            shape((tall, hidden), BF),
            shape((tall, hidden), BF),
            shape((tall, depth), BF),
            shape((tall, depth), BF),
        ],
        in_specs=[vmem, vmem, anywhere, anywhere],
        out_specs=[vmem, vmem, anywhere, anywhere, anywhere, anywhere],
        scratch_shapes=[pltpu.VMEM((2, tall >> j, width), BF) for j in range(levels)]
        + [pltpu.VMEM((RING, tall >> (j + 1), width), BF) for j in range(levels)]
        + [
            pltpu.VMEM((RING, tall, width), BF),
            pltpu.VMEM((chunks, depth, width), BF),
            pltpu.VMEM((chunks, width, depth), BF),
            pltpu.VMEM((tall, depth), BF),
            pltpu.VMEM((tall, depth), BF),
            pltpu.VMEM((chunks, tall >> levels, width), F32),
            pltpu.VMEM((tall, depth), F32),
            dma((levels, 2)),
            dma((levels, RING)),
            dma((levels, 2)),
            dma((levels, RING)),
            dma((2, 2, n_row)),
            dma((2, 2, n_row)),
            dma((2, chunks)),
            dma((2,)),
            dma((2,)),
        ],
        compiler_params=pltpu.CompilerParams(
            collective_id=0, has_side_effects=True, vmem_limit_bytes=58 * 2**20
        ),
        cost_estimate=pl.CostEstimate(
            flops=flops, bytes_accessed=8 * depth * hidden, transcendentals=0
        ),
    )(page_tokens, upstream, weight_in, weight_out)


def shards(n_row, n_col, page_tokens, weight_in, weight_out, upstream):
    block_part, token_part, active, grad_hidden, features, upstream_all = encode(
        n_row, n_col, page_tokens, upstream, weight_in, weight_out
    )
    block_out = lax.psum_scatter(block_part, "row", scatter_dimension=0, tiled=True)
    grad_tokens = lax.psum_scatter(token_part, "row", scatter_dimension=0, tiled=True)
    grad_weight_in = contract_first(features, grad_hidden).astype(BF)
    grad_weight_out = contract_first(active, upstream_all).astype(BF)
    return (block_out, grad_tokens, grad_weight_in, grad_weight_out)


def solution(mesh):
    placed = (P("row", "col"), P("col", "row"), P("row", "col"), P("row", "col"))
    return jax.shard_map(
        functools.partial(shards, mesh.shape["row"], mesh.shape["col"]),
        mesh=mesh,
        in_specs=placed,
        out_specs=(P("row", "col"), P("row", "col"), P("col", "row"), P("row", "col")),
        check_vma=False,
    )
```

```python
import functools

import jax
import jax.numpy as jnp
from jax import lax
from jax.experimental import pallas as pl
from jax.experimental.pallas import tpu as pltpu
from jax.sharding import PartitionSpec as P

MESH = pl.DeviceIdType.MESH
RING = 12
BF = jnp.bfloat16
F32 = jnp.float32


def activate(values):
    return (
        0.5
        * values
        * (1.0 + jnp.tanh(0.7978845608 * (values + 0.044715 * values * values * values)))
    )


def slope(values):
    square = values * values
    bend = jnp.tanh(0.7978845608 * (values + 0.044715 * square * values))
    return 0.5 * (1.0 + bend) + 0.5 * values * (1.0 - bend * bend) * (
        0.7978845608 * (1.0 + 0.134145 * square)
    )


def contract_last(left, right):
    return lax.dot_general(left, right, (((1,), (1,)), ((), ())), preferred_element_type=F32)


def contract_first(left, right):
    return lax.dot_general(left, right, (((0,), (0,)), ((), ())), preferred_element_type=F32)


def kernel(
    n_row,
    n_col,
    tokens_ref,
    upstream_ref,
    weight_in,
    weight_out,
    block_out,
    token_part,
    active_out,
    hidden_out,
    features_out,
    upstream_out,
    *scratch,
):
    levels = n_col.bit_length() - 1
    piles = scratch[: levels]
    landed = scratch[levels : 2 * levels]
    (
        gathered,
        held_in,
        held_out,
        features,
        upstream,
        pre,
        total,
        stage_send,
        stage_recv,
        spread_send,
        spread_recv,
        row_send,
        row_recv,
        weight_sem,
        out_sem,
        side_sem,
        block_part,
        block_landed,
        block_send,
        block_recv,
    ) = scratch[2 * levels :]
    chunks, depth, width = held_in.shape
    tall = features.shape[0]
    rows = tokens_ref.shape[0]
    steps = 2 * chunks
    here = lax.axis_index("row")
    me = lax.axis_index("col")

    bits = [(me // 2**j) % 2 for j in range(levels)]
    strides = [2**j for j in range(levels)]
    if levels == 3:
        core, bx, by = bits
        bits = [core, bx * (1 - core) + by * core, by * (1 - core) + bx * core]
        strides = [1, 2 + 2 * core, 4 - 2 * core]
    mates = [me + s * (1 - 2 * b) for s, b in zip(strides, bits)]
    sizes = [tall >> (j + 1) for j in range(levels)]
    starts = [0]
    for j in range(levels):
        starts.append(starts[-1] + bits[j] * sizes[j])

    barrier = pltpu.get_barrier_semaphore()
    for mate in mates:
        pl.semaphore_signal(barrier, inc=1, device_id=(here, mate), device_id_type=MESH)

    for d in range(1, n_row):
        pl.semaphore_signal(
            barrier, inc=1, device_id=(lax.rem(here + d, n_row), me), device_id_type=MESH
        )

    def load_in(k):
        return pltpu.make_async_copy(
            weight_in.at[:, pl.ds(pl.multiple_of(k * width, width), width)],
            held_in.at[k],
            weight_sem.at[0, k],
        )

    def load_out(k):
        return pltpu.make_async_copy(
            weight_out.at[pl.ds(pl.multiple_of(k * width, width), width), :],
            held_out.at[k],
            weight_sem.at[1, k],
        )

    @pl.loop(0, chunks)
    def _(k):
        load_in(k).start()

    sources = (tokens_ref, upstream_ref)
    whole = (features, upstream)

    def block_of(kind, origin):
        return whole[kind].at[pl.ds(pl.multiple_of(origin * rows, rows), rows), :]

    def hop(kind, way, dist):
        origin = here - dist if way == 0 else here + dist
        goal = here + 1 if way == 0 else here - 1
        source = sources[kind] if dist == 0 else block_of(kind, origin)
        return pltpu.make_async_remote_copy(
            src_ref=source,
            dst_ref=block_of(kind, origin),
            send_sem=row_send.at[kind, way, dist],
            recv_sem=row_recv.at[kind, way, dist],
            device_id=(goal, me),
            device_id_type=MESH,
        )

    def sends(way, dist):
        if way == 0:
            return (here >= dist) & (here < n_row - 1)
        return (here < n_row - dist) & (here > 0)

    def takes(way, dist):
        return here >= dist + 1 if way == 0 else here < n_row - dist - 1

    def arrive(kind, dist):
        for way in (0, 1):

            @pl.when(takes(way, dist))
            def _(way=way):
                origin = here - dist - 1 if way == 0 else here + dist + 1
                pltpu.make_async_remote_copy(
                    src_ref=block_of(kind, origin),
                    dst_ref=block_of(kind, origin),
                    send_sem=row_send.at[kind, way, dist],
                    recv_sem=row_recv.at[kind, way, dist],
                    device_id=(here - 1 if way == 0 else here + 1, me),
                    device_id_type=MESH,
                ).wait_recv()

            if dist + 1 < n_row - 1:

                @pl.when(sends(way, dist + 1))
                def _(way=way):
                    hop(kind, way, dist + 1).start()

    pl.semaphore_wait(barrier, levels + n_row - 1)

    def open_rows(kind):
        for way in (0, 1):

            @pl.when(sends(way, 0))
            def _(way=way):
                hop(kind, way, 0).start()

    def hand_over(d):
        goal = lax.rem(here + d, n_row)
        return pltpu.make_async_remote_copy(
            src_ref=block_part.at[pl.ds(pl.multiple_of(goal * rows, rows), rows), :],
            dst_ref=block_landed.at[d - 1],
            send_sem=block_send.at[d - 1],
            recv_sem=block_recv.at[d - 1],
            device_id=(goal, me),
            device_id_type=MESH,
        )

    open_rows(0)

    @pl.loop(0, chunks)
    def _(k):
        load_out(k).start()

    own = pl.ds(pl.multiple_of(here * rows, rows), rows)
    features[own, :] = tokens_ref[...]
    upstream[own, :] = upstream_ref[...]
    for dist in range(n_row - 1):
        arrive(0, dist)
    open_rows(1)
    pltpu.make_async_copy(features, features_out, side_sem.at[0]).start()

    def stage(j, t):
        other = pl.multiple_of((1 - bits[j]) * sizes[j], sizes[j])
        return pltpu.make_async_remote_copy(
            src_ref=piles[j].at[lax.rem(t, 2), pl.ds(other, sizes[j]), :],
            dst_ref=landed[j].at[lax.rem(t, RING)],
            send_sem=stage_send.at[j, lax.rem(t, 2)],
            recv_sem=stage_recv.at[j, lax.rem(t, RING)],
            device_id=(here, mates[j]),
            device_id_type=MESH,
        )

    def spread(j, t, mine=True):
        at = starts[j + 1] if mine else starts[j] + (1 - bits[j]) * sizes[j]
        view = gathered.at[lax.rem(t, RING), pl.ds(pl.multiple_of(at, sizes[j]), sizes[j]), :]
        return pltpu.make_async_remote_copy(
            src_ref=view,
            dst_ref=view,
            send_sem=spread_send.at[j, lax.rem(t, 2)],
            recv_sem=spread_recv.at[j, lax.rem(t, RING)],
            device_id=(here, mates[j]),
            device_id_type=MESH,
        )

    def columns(k):
        return pl.ds(pl.multiple_of(k * width, width), width)

    def put_active(t):
        return pltpu.make_async_copy(
            gathered.at[lax.rem(t, RING)], active_out.at[:, columns(t)], out_sem.at[lax.rem(t, 2)]
        )

    def put_hidden(t):
        return pltpu.make_async_copy(
            gathered.at[lax.rem(t, RING)],
            hidden_out.at[:, columns(t - chunks)],
            out_sem.at[lax.rem(t, 2)],
        )

    tile = min(512, tall)

    def during(t, act):
        pl.when((t >= 0) & (t < steps))(act)

    def produce(t):
        slot = lax.rem(t, 2)

        @pl.when(t < chunks)
        def _():
            load_in(t).wait()

            @pl.loop(0, tall // tile)
            def _(r):
                at = pl.ds(pl.multiple_of(r * tile, tile), tile)
                piles[0][slot, at, :] = jnp.dot(
                    features[at, :], held_in[t], preferred_element_type=F32
                ).astype(BF)

        @pl.when(t >= chunks)
        def _():
            @pl.loop(0, tall // tile)
            def _(r):
                at = pl.ds(pl.multiple_of(r * tile, tile), tile)
                piles[0][slot, at, :] = contract_last(
                    upstream[at, :], held_out[t - chunks]
                ).astype(BF)

        stage(0, t).start()

    def fold(j, t):
        copy = stage(j, t)
        copy.wait_send()
        copy.wait_recv()
        slot, ring = lax.rem(t, 2), lax.rem(t, RING)
        part = min(32, sizes[j])
        keep = bits[j] * sizes[j]

        if j < levels - 1:
            def combine(r):
                at = pl.ds(pl.multiple_of(r * part, part), part)
                held = pl.ds(pl.multiple_of(keep + r * part, part), part)
                piles[j + 1][slot, at, :] = (
                    piles[j][slot, held, :].astype(F32) + landed[j][ring, at, :].astype(F32)
                ).astype(BF)

            count = sizes[j + 1] // part
            other = (1 - bits[j + 1]) * count

            @pl.loop(0, count)
            def _(r):
                combine(other + r)

            stage(j + 1, t).start()
            mine = bits[j + 1] * count

            @pl.loop(0, count)
            def _(r):
                combine(mine + r)
        else:
            k = lax.rem(t, chunks)

            @pl.loop(0, sizes[j] // part)
            def _(r):
                at = pl.ds(pl.multiple_of(r * part, part), part)
                held = pl.ds(pl.multiple_of(keep + r * part, part), part)
                target = pl.ds(pl.multiple_of(starts[levels] + r * part, part), part)
                value = piles[j][slot, held, :].astype(F32) + landed[j][ring, at, :].astype(F32)

                @pl.when(t < chunks)
                def _():
                    pre[k, at, :] = value
                    gathered[ring, target, :] = activate(value).astype(BF)

                @pl.when(t >= chunks)
                def _():
                    gathered[ring, target, :] = (value * slope(pre[k, at, :])).astype(BF)

            spread(j, t).start()

    def gather(j, t):
        spread(j, t).wait_send()
        spread(j, t, mine=False).wait_recv()
        spread(j - 1, t).start()

    def consume(t):
        spread(0, t).wait_send()
        spread(0, t, mine=False).wait_recv()
        ring = lax.rem(t, RING)
        k = lax.rem(t, chunks)

        @pl.when(k == 0)
        def _():
            total[...] = jnp.zeros_like(total)

        @pl.when(t < chunks)
        def _():
            put_active(t).start()
            load_out(t).wait()

            @pl.loop(0, tall // tile)
            def _(r):
                at = pl.ds(pl.multiple_of(r * tile, tile), tile)
                total[at, :] += jnp.dot(
                    gathered[ring, at, :], held_out[t], preferred_element_type=F32
                )

        @pl.when(t >= chunks)
        def _():
            put_hidden(t).start()

            @pl.loop(0, tall // tile)
            def _(r):
                at = pl.ds(pl.multiple_of(r * tile, tile), tile)
                total[at, :] += contract_last(gathered[ring, at, :], held_in[t - chunks])

        @pl.when(t == chunks - 1)
        def _():
            block_part[...] = total[...].astype(BF)
            for d in range(1, n_row):
                hand_over(d).start()

        @pl.when(t == steps - 1)
        def _():
            token_part[...] = total[...].astype(BF)

    def written(t):
        @pl.when(t < chunks)
        def _():
            put_active(t).wait()

        @pl.when(t >= chunks)
        def _():
            put_hidden(t).wait()

    folds = [1 + 2 * j for j in range(levels)]
    gathers = [folds[-1] + 2 * (levels - j) for j in range(levels)]
    lag = gathers[1] + 1
    pace = max(1, (chunks - 1) // n_row)

    @pl.loop(0, steps + lag + 1)
    def _(i):
        during(i - lag - 1, lambda: written(i - lag - 1))
        during(i - lag, lambda: consume(i - lag))
        for j in range(1, levels):
            during(i - gathers[j], functools.partial(gather, j, i - gathers[j]))
        for j in range(levels - 1, -1, -1):
            during(i - folds[j], functools.partial(fold, j, i - folds[j]))
        during(i, lambda: produce(i))
        for dist in range(n_row - 1):

            @pl.when(i == pace * (dist + 1))
            def _(dist=dist):
                arrive(1, dist)

    side = pltpu.make_async_copy(upstream, upstream_out, side_sem.at[1])
    side.start()
    part = min(32, rows)
    for d in range(1, n_row):
        hand_over(d).wait()

    @pl.loop(0, rows // part)
    def _(r):
        at = pl.ds(pl.multiple_of(r * part, part), part)
        held = pl.ds(pl.multiple_of(here * rows + r * part, part), part)
        value = block_part[held, :].astype(F32)
        for d in range(1, n_row):
            value += block_landed[d - 1, at, :].astype(F32)
        block_out[at, :] = value.astype(BF)

    side.wait()
    pltpu.make_async_copy(features, features_out, side_sem.at[0]).wait()
    for kind in (0, 1):
        for dist in range(n_row - 1):
            for way in (0, 1):

                @pl.when(sends(way, dist))
                def _(kind=kind, way=way, dist=dist):
                    hop(kind, way, dist).wait_send()


def encode(n_row, n_col, page_tokens, upstream, weight_in, weight_out):
    rows, depth = page_tokens.shape
    hidden = weight_in.shape[1]
    tall = rows * n_row
    levels = n_col.bit_length() - 1
    chunks = 14
    width = hidden // chunks
    vmem = pl.BlockSpec(memory_space=pltpu.VMEM)
    anywhere = pl.BlockSpec(memory_space=pl.ANY)
    dma = pltpu.SemaphoreType.DMA
    shape = jax.ShapeDtypeStruct
    flops = 8 * tall * depth * hidden
    return pl.pallas_call(
        functools.partial(kernel, n_row, n_col),
        out_shape=[
            shape((rows, depth), BF),
            shape((tall, depth), BF),
            shape((tall, hidden), BF),
            shape((tall, hidden), BF),
            shape((tall, depth), BF),
            shape((tall, depth), BF),
        ],
        in_specs=[vmem, vmem, anywhere, anywhere],
        out_specs=[vmem, vmem, anywhere, anywhere, anywhere, anywhere],
        scratch_shapes=[pltpu.VMEM((2, tall >> j, width), BF) for j in range(levels)]
        + [pltpu.VMEM((RING, tall >> (j + 1), width), BF) for j in range(levels)]
        + [
            pltpu.VMEM((RING, tall, width), BF),
            pltpu.VMEM((chunks, depth, width), BF),
            pltpu.VMEM((chunks, width, depth), BF),
            pltpu.VMEM((tall, depth), BF),
            pltpu.VMEM((tall, depth), BF),
            pltpu.VMEM((chunks, tall >> levels, width), F32),
            pltpu.VMEM((tall, depth), F32),
            dma((levels, 2)),
            dma((levels, RING)),
            dma((levels, 2)),
            dma((levels, RING)),
            dma((2, 2, n_row)),
            dma((2, 2, n_row)),
            dma((2, chunks)),
            dma((2,)),
            dma((2,)),
            pltpu.VMEM((tall, depth), BF),
            pltpu.VMEM((n_row - 1, rows, depth), BF),
            dma((n_row - 1,)),
            dma((n_row - 1,)),
        ],
        compiler_params=pltpu.CompilerParams(
            collective_id=0, has_side_effects=True, vmem_limit_bytes=58 * 2**20
        ),
        cost_estimate=pl.CostEstimate(
            flops=flops, bytes_accessed=8 * depth * hidden, transcendentals=0
        ),
    )(page_tokens, upstream, weight_in, weight_out)


def shards(n_row, n_col, page_tokens, weight_in, weight_out, upstream):
    block_out, token_part, active, grad_hidden, features, upstream_all = encode(
        n_row, n_col, page_tokens, upstream, weight_in, weight_out
    )
    grad_tokens = lax.psum_scatter(token_part, "row", scatter_dimension=0, tiled=True)
    grad_weight_in = contract_first(features, grad_hidden).astype(BF)
    grad_weight_out = contract_first(active, upstream_all).astype(BF)
    return (block_out, grad_tokens, grad_weight_in, grad_weight_out)


def solution(mesh):
    placed = (P("row", "col"), P("col", "row"), P("row", "col"), P("row", "col"))
    return jax.shard_map(
        functools.partial(shards, mesh.shape["row"], mesh.shape["col"]),
        mesh=mesh,
        in_specs=placed,
        out_specs=(P("row", "col"), P("row", "col"), P("col", "row"), P("row", "col")),
        check_vma=False,
    )
```

```python
import functools

import jax
import jax.numpy as jnp
from jax import lax
from jax.experimental import pallas as pl
from jax.experimental.pallas import tpu as pltpu
from jax.sharding import PartitionSpec as P

MESH = pl.DeviceIdType.MESH
RING = 12
BF = jnp.bfloat16
F32 = jnp.float32


def activate(values):
    return (
        0.5
        * values
        * (1.0 + jnp.tanh(0.7978845608 * (values + 0.044715 * values * values * values)))
    )


def slope(values):
    square = values * values
    bend = jnp.tanh(0.7978845608 * (values + 0.044715 * square * values))
    return 0.5 * (1.0 + bend) + 0.5 * values * (1.0 - bend * bend) * (
        0.7978845608 * (1.0 + 0.134145 * square)
    )


def contract_last(left, right):
    return lax.dot_general(left, right, (((1,), (1,)), ((), ())), preferred_element_type=F32)


def contract_first(left, right):
    return lax.dot_general(left, right, (((0,), (0,)), ((), ())), preferred_element_type=F32)


def kernel(
    n_row,
    n_col,
    tokens_ref,
    upstream_ref,
    weight_in,
    weight_out,
    block_out,
    active_out,
    hidden_out,
    features_out,
    upstream_out,
    *scratch,
):
    token_parts, scratch = scratch[:n_row], scratch[n_row:]
    levels = n_col.bit_length() - 1
    piles = scratch[: levels]
    landed = scratch[levels : 2 * levels]
    (
        gathered,
        held_in,
        held_out,
        features,
        upstream,
        pre,
        total,
        stage_send,
        stage_recv,
        spread_send,
        spread_recv,
        row_send,
        row_recv,
        weight_sem,
        out_sem,
        side_sem,
        block_part,
        block_landed,
        block_send,
        block_recv,
    ) = scratch[2 * levels :]
    chunks, depth, width = held_in.shape
    tall = features.shape[0]
    rows = tokens_ref.shape[0]
    steps = 2 * chunks
    here = lax.axis_index("row")
    me = lax.axis_index("col")

    bits = [(me // 2**j) % 2 for j in range(levels)]
    strides = [2**j for j in range(levels)]
    if levels == 3:
        core, bx, by = bits
        bits = [core, bx * (1 - core) + by * core, by * (1 - core) + bx * core]
        strides = [1, 2 + 2 * core, 4 - 2 * core]
    mates = [me + s * (1 - 2 * b) for s, b in zip(strides, bits)]
    sizes = [tall >> (j + 1) for j in range(levels)]
    starts = [0]
    for j in range(levels):
        starts.append(starts[-1] + bits[j] * sizes[j])

    barrier = pltpu.get_barrier_semaphore()
    for mate in mates:
        pl.semaphore_signal(barrier, inc=1, device_id=(here, mate), device_id_type=MESH)

    for d in range(1, n_row):
        pl.semaphore_signal(
            barrier, inc=1, device_id=(lax.rem(here + d, n_row), me), device_id_type=MESH
        )

    def load_in(k):
        return pltpu.make_async_copy(
            weight_in.at[:, pl.ds(pl.multiple_of(k * width, width), width)],
            held_in.at[k],
            weight_sem.at[0, k],
        )

    def load_out(k):
        return pltpu.make_async_copy(
            weight_out.at[pl.ds(pl.multiple_of(k * width, width), width), :],
            held_out.at[k],
            weight_sem.at[1, k],
        )

    @pl.loop(0, chunks)
    def _(k):
        load_in(k).start()

    sources = (tokens_ref, upstream_ref)
    whole = (features, upstream)

    def block_of(kind, origin):
        return whole[kind].at[pl.ds(pl.multiple_of(origin * rows, rows), rows), :]

    def hop(kind, way, dist):
        origin = here - dist if way == 0 else here + dist
        goal = here + 1 if way == 0 else here - 1
        source = sources[kind] if dist == 0 else block_of(kind, origin)
        return pltpu.make_async_remote_copy(
            src_ref=source,
            dst_ref=block_of(kind, origin),
            send_sem=row_send.at[kind, way, dist],
            recv_sem=row_recv.at[kind, way, dist],
            device_id=(goal, me),
            device_id_type=MESH,
        )

    def sends(way, dist):
        if way == 0:
            return (here >= dist) & (here < n_row - 1)
        return (here < n_row - dist) & (here > 0)

    def takes(way, dist):
        return here >= dist + 1 if way == 0 else here < n_row - dist - 1

    def arrive(kind, dist):
        for way in (0, 1):

            @pl.when(takes(way, dist))
            def _(way=way):
                origin = here - dist - 1 if way == 0 else here + dist + 1
                pltpu.make_async_remote_copy(
                    src_ref=block_of(kind, origin),
                    dst_ref=block_of(kind, origin),
                    send_sem=row_send.at[kind, way, dist],
                    recv_sem=row_recv.at[kind, way, dist],
                    device_id=(here - 1 if way == 0 else here + 1, me),
                    device_id_type=MESH,
                ).wait_recv()

            if dist + 1 < n_row - 1:

                @pl.when(sends(way, dist + 1))
                def _(way=way):
                    hop(kind, way, dist + 1).start()

    pl.semaphore_wait(barrier, levels + n_row - 1)

    def open_rows(kind):
        for way in (0, 1):

            @pl.when(sends(way, 0))
            def _(way=way):
                hop(kind, way, 0).start()

    def hand_over(d):
        goal = lax.rem(here + d, n_row)
        return pltpu.make_async_remote_copy(
            src_ref=block_part.at[pl.ds(pl.multiple_of(goal * rows, rows), rows), :],
            dst_ref=block_landed.at[d - 1],
            send_sem=block_send.at[d - 1],
            recv_sem=block_recv.at[d - 1],
            device_id=(goal, me),
            device_id_type=MESH,
        )

    open_rows(0)

    @pl.loop(0, chunks)
    def _(k):
        load_out(k).start()

    own = pl.ds(pl.multiple_of(here * rows, rows), rows)
    features[own, :] = tokens_ref[...]
    upstream[own, :] = upstream_ref[...]
    for dist in range(n_row - 1):
        arrive(0, dist)
    open_rows(1)
    pltpu.make_async_copy(features, features_out, side_sem.at[0]).start()

    def stage(j, t):
        other = pl.multiple_of((1 - bits[j]) * sizes[j], sizes[j])
        return pltpu.make_async_remote_copy(
            src_ref=piles[j].at[lax.rem(t, 2), pl.ds(other, sizes[j]), :],
            dst_ref=landed[j].at[lax.rem(t, RING)],
            send_sem=stage_send.at[j, lax.rem(t, 2)],
            recv_sem=stage_recv.at[j, lax.rem(t, RING)],
            device_id=(here, mates[j]),
            device_id_type=MESH,
        )

    def spread(j, t, mine=True):
        at = starts[j + 1] if mine else starts[j] + (1 - bits[j]) * sizes[j]
        view = gathered.at[lax.rem(t, RING), pl.ds(pl.multiple_of(at, sizes[j]), sizes[j]), :]
        return pltpu.make_async_remote_copy(
            src_ref=view,
            dst_ref=view,
            send_sem=spread_send.at[j, lax.rem(t, 2)],
            recv_sem=spread_recv.at[j, lax.rem(t, RING)],
            device_id=(here, mates[j]),
            device_id_type=MESH,
        )

    def columns(k):
        return pl.ds(pl.multiple_of(k * width, width), width)

    def put_active(t):
        return pltpu.make_async_copy(
            gathered.at[lax.rem(t, RING)], active_out.at[:, columns(t)], out_sem.at[lax.rem(t, 2)]
        )

    def put_hidden(t):
        return pltpu.make_async_copy(
            gathered.at[lax.rem(t, RING)],
            hidden_out.at[:, columns(t - chunks)],
            out_sem.at[lax.rem(t, 2)],
        )

    tile = min(512, tall)

    def during(t, act):
        pl.when((t >= 0) & (t < steps))(act)

    def produce(t):
        slot = lax.rem(t, 2)

        @pl.when(t < chunks)
        def _():
            load_in(t).wait()

            @pl.loop(0, tall // tile)
            def _(r):
                at = pl.ds(pl.multiple_of(r * tile, tile), tile)
                piles[0][slot, at, :] = jnp.dot(
                    features[at, :], held_in[t], preferred_element_type=F32
                ).astype(BF)

        @pl.when(t >= chunks)
        def _():
            @pl.loop(0, tall // tile)
            def _(r):
                at = pl.ds(pl.multiple_of(r * tile, tile), tile)
                piles[0][slot, at, :] = contract_last(
                    upstream[at, :], held_out[t - chunks]
                ).astype(BF)

        stage(0, t).start()

    def fold(j, t):
        copy = stage(j, t)
        copy.wait_send()
        copy.wait_recv()
        slot, ring = lax.rem(t, 2), lax.rem(t, RING)
        part = min(32, sizes[j])
        keep = bits[j] * sizes[j]

        if j < levels - 1:
            def combine(r):
                at = pl.ds(pl.multiple_of(r * part, part), part)
                held = pl.ds(pl.multiple_of(keep + r * part, part), part)
                piles[j + 1][slot, at, :] = (
                    piles[j][slot, held, :].astype(F32) + landed[j][ring, at, :].astype(F32)
                ).astype(BF)

            count = sizes[j + 1] // part
            other = (1 - bits[j + 1]) * count

            @pl.loop(0, count)
            def _(r):
                combine(other + r)

            stage(j + 1, t).start()
            mine = bits[j + 1] * count

            @pl.loop(0, count)
            def _(r):
                combine(mine + r)
        else:
            k = lax.rem(t, chunks)

            @pl.loop(0, sizes[j] // part)
            def _(r):
                at = pl.ds(pl.multiple_of(r * part, part), part)
                held = pl.ds(pl.multiple_of(keep + r * part, part), part)
                target = pl.ds(pl.multiple_of(starts[levels] + r * part, part), part)
                value = piles[j][slot, held, :].astype(F32) + landed[j][ring, at, :].astype(F32)

                @pl.when(t < chunks)
                def _():
                    pre[k, at, :] = value
                    gathered[ring, target, :] = activate(value).astype(BF)

                @pl.when(t >= chunks)
                def _():
                    gathered[ring, target, :] = (value * slope(pre[k, at, :])).astype(BF)

            spread(j, t).start()

    def gather(j, t):
        spread(j, t).wait_send()
        spread(j, t, mine=False).wait_recv()
        spread(j - 1, t).start()

    def consume(t):
        spread(0, t).wait_send()
        spread(0, t, mine=False).wait_recv()
        ring = lax.rem(t, RING)
        k = lax.rem(t, chunks)

        @pl.when(k == 0)
        def _():
            total[...] = jnp.zeros_like(total)

        @pl.when(t < chunks)
        def _():
            put_active(t).start()
            load_out(t).wait()

            @pl.loop(0, tall // tile)
            def _(r):
                at = pl.ds(pl.multiple_of(r * tile, tile), tile)
                total[at, :] += jnp.dot(
                    gathered[ring, at, :], held_out[t], preferred_element_type=F32
                )

        @pl.when(t >= chunks)
        def _():
            put_hidden(t).start()

            @pl.loop(0, tall // tile)
            def _(r):
                at = pl.ds(pl.multiple_of(r * tile, tile), tile)
                total[at, :] += contract_last(gathered[ring, at, :], held_in[t - chunks])

        @pl.when(t == chunks - 1)
        def _():
            block_part[...] = total[...].astype(BF)
            for d in range(1, n_row):
                hand_over(d).start()

        @pl.when(t == steps - 1)
        def _():
            for d in range(n_row):
                goal = lax.rem(here + d, n_row)
                token_parts[d][...] = total[
                    pl.ds(pl.multiple_of(goal * rows, rows), rows), :
                ].astype(BF)

    def written(t):
        @pl.when(t < chunks)
        def _():
            put_active(t).wait()

        @pl.when(t >= chunks)
        def _():
            put_hidden(t).wait()

    folds = [1 + 2 * j for j in range(levels)]
    gathers = [folds[-1] + 2 * (levels - j) for j in range(levels)]
    lag = gathers[1] + 1
    pace = max(1, (chunks - 1) // n_row)

    @pl.loop(0, steps + lag + 1)
    def _(i):
        during(i - lag - 1, lambda: written(i - lag - 1))
        during(i - lag, lambda: consume(i - lag))
        for j in range(1, levels):
            during(i - gathers[j], functools.partial(gather, j, i - gathers[j]))
        for j in range(levels - 1, -1, -1):
            during(i - folds[j], functools.partial(fold, j, i - folds[j]))
        during(i, lambda: produce(i))
        for dist in range(n_row - 1):

            @pl.when(i == pace * (dist + 1))
            def _(dist=dist):
                arrive(1, dist)

    side = pltpu.make_async_copy(upstream, upstream_out, side_sem.at[1])
    side.start()
    part = min(32, rows)
    for d in range(1, n_row):
        hand_over(d).wait()

    @pl.loop(0, rows // part)
    def _(r):
        at = pl.ds(pl.multiple_of(r * part, part), part)
        held = pl.ds(pl.multiple_of(here * rows + r * part, part), part)
        value = block_part[held, :].astype(F32)
        for d in range(1, n_row):
            value += block_landed[d - 1, at, :].astype(F32)
        block_out[at, :] = value.astype(BF)

    side.wait()
    pltpu.make_async_copy(features, features_out, side_sem.at[0]).wait()
    for kind in (0, 1):
        for dist in range(n_row - 1):
            for way in (0, 1):

                @pl.when(sends(way, dist))
                def _(kind=kind, way=way, dist=dist):
                    hop(kind, way, dist).wait_send()


def encode(n_row, n_col, page_tokens, upstream, weight_in, weight_out):
    rows, depth = page_tokens.shape
    hidden = weight_in.shape[1]
    tall = rows * n_row
    levels = n_col.bit_length() - 1
    chunks = 14
    width = hidden // chunks
    vmem = pl.BlockSpec(memory_space=pltpu.VMEM)
    anywhere = pl.BlockSpec(memory_space=pl.ANY)
    dma = pltpu.SemaphoreType.DMA
    shape = jax.ShapeDtypeStruct
    flops = 8 * tall * depth * hidden
    return pl.pallas_call(
        functools.partial(kernel, n_row, n_col),
        out_shape=[
            shape((rows, depth), BF),
            shape((tall, hidden), BF),
            shape((tall, hidden), BF),
            shape((tall, depth), BF),
            shape((tall, depth), BF),
        ]
        + [shape((rows, depth), BF)] * n_row,
        in_specs=[vmem, vmem, anywhere, anywhere],
        out_specs=[vmem, anywhere, anywhere, anywhere, anywhere] + [vmem] * n_row,
        scratch_shapes=[pltpu.VMEM((2, tall >> j, width), BF) for j in range(levels)]
        + [pltpu.VMEM((RING, tall >> (j + 1), width), BF) for j in range(levels)]
        + [
            pltpu.VMEM((RING, tall, width), BF),
            pltpu.VMEM((chunks, depth, width), BF),
            pltpu.VMEM((chunks, width, depth), BF),
            pltpu.VMEM((tall, depth), BF),
            pltpu.VMEM((tall, depth), BF),
            pltpu.VMEM((chunks, tall >> levels, width), F32),
            pltpu.VMEM((tall, depth), F32),
            dma((levels, 2)),
            dma((levels, RING)),
            dma((levels, 2)),
            dma((levels, RING)),
            dma((2, 2, n_row)),
            dma((2, 2, n_row)),
            dma((2, chunks)),
            dma((2,)),
            dma((2,)),
            pltpu.VMEM((tall, depth), BF),
            pltpu.VMEM((n_row - 1, rows, depth), BF),
            dma((n_row - 1,)),
            dma((n_row - 1,)),
        ],
        compiler_params=pltpu.CompilerParams(
            collective_id=0, has_side_effects=True, vmem_limit_bytes=58 * 2**20
        ),
        cost_estimate=pl.CostEstimate(
            flops=flops, bytes_accessed=8 * depth * hidden, transcendentals=0
        ),
    )(page_tokens, upstream, weight_in, weight_out)


def shards(n_row, n_col, page_tokens, weight_in, weight_out, upstream):
    block_out, active, grad_hidden, features, upstream_all, *parts = encode(
        n_row, n_col, page_tokens, upstream, weight_in, weight_out
    )
    moved = [
        lax.ppermute(parts[d], "row", [(i, (i + d) % n_row) for i in range(n_row)])
        for d in range(n_row - 1, 0, -1)
    ]
    grad_weight_in = contract_first(features, grad_hidden).astype(BF)
    grad_weight_out = contract_first(active, upstream_all).astype(BF)
    total = parts[0].astype(F32)
    for piece in moved:
        total = total + piece.astype(F32)
    grad_tokens = total.astype(BF)
    return (block_out, grad_tokens, grad_weight_in, grad_weight_out)


def solution(mesh):
    placed = (P("row", "col"), P("col", "row"), P("row", "col"), P("row", "col"))
    return jax.shard_map(
        functools.partial(shards, mesh.shape["row"], mesh.shape["col"]),
        mesh=mesh,
        in_specs=placed,
        out_specs=(P("row", "col"), P("row", "col"), P("col", "row"), P("row", "col")),
        check_vma=False,
    )
```
